32 devices in a mesh: dp: 16 (over z, x, core), mp: 2 (over y).
Axes of the slice: x: 2, y: 2, z: 4, core: 2. Of those that a mesh axis runs over, the one named last changes fastest.
Arguments:
- corpus: bfloat16 [2048, 16, 320], P('dp'), may hold values from -6 to 6
- picks: int32 [16, 16], P('dp'), may hold values from 0 to 127
- lengths: int32 [2048], P('dp'), may hold values from 1 to 16, 24576 in all
- langs: int32 [2048], P('dp'), may hold values from 0 to 127
- w_in: bfloat16 [320, 1536], P(None, 'mp'), may hold values from -0.3125 to 0.3125
- lang_table: bfloat16 [128, 1536], P(None, 'mp'), may hold values from -3 to 3
- ln_gain: float32 [1536], P('mp'), may hold values from 0.1 to 1.9
- w_pw1: bfloat16 [1536, 2, 1536], P('dp', None, 'mp'), may hold values from -0.15625 to 0.15625
- kernel: float32 [31, 1536], P(None, 'mp'), may hold values from -1.5 to 1.5
- bn_gain: float32 [1536], P('mp'), may hold values from 0.1 to 1.9
- bn_bias: float32 [1536], P('mp'), may hold values from -3 to 3
- w_pw2: bfloat16 [1536, 1536], P('dp', 'mp'), may hold values from -0.15625 to 0.15625
- cotangent: bfloat16 [4096, 1536], P('dp', 'mp'), may hold values from -6 to 6
Outputs:
- encoded: bfloat16 [4096, 1536], P('dp', 'mp')
- grad_pw1: float32 [1536, 2, 1536], P('dp', None, 'mp')
- grad_pw2: float32 [1536, 1536], P('dp', 'mp')
- grad_kernel: float32 [31, 1536], P(None, 'mp')
- grad_bn_gain: float32 [1536], P('mp')
- grad_bn_bias: float32 [1536], P('mp')
The draws below stay inside these ranges and needn't reach their ends.
Inputs may be any that keep to these rules, and one draw needn't show every extreme that they name: `picks`: each trainer takes one block of every shard; a shard may give the same block to several trainers.
All inputs are finite; a program needn't handle non-finite values. No bound on the sum of `lengths` on one device may be relied on, other than what follows from the above.
Results may differ from the reference program's by a relative error of at most 0.0057.
Values may be sent and summed in bfloat16 or wider, within the bound.
A program may use at most 64 MiB of HBM per device.

```python
import math
import jax
import jax.numpy as jnp
import numpy as np
from jax import lax

D = 1536
FEAT = 320
LANGS = 128
KER = 31
BLK = 16
CB = 128
TOTAL_ROWS = 4096
CORPUS = 2048
N_DP = 16


def with_ends(entries, key, smallest, top_value):
    longest = entries.shape.index(max(entries.shape))
    spots = []
    for shift in (0, 1):
        where = [jax.random.randint(jax.random.fold_in(key, axis), (), 0, length) for axis, length in enumerate(entries.shape)]
        where[longest] = (where[longest] + shift) % entries.shape[longest]
        spots.append(tuple(where))
    return entries.at[spots[0]].set(smallest).at[spots[1]].set(top_value)


def block_scale(own_key, dims, split, smallest, largest):
    level, own = 1.0, jax.random.fold_in(own_key, 6)
    for axis_at, shards_of in split:
        steps = jnp.exp(jax.random.uniform(jax.random.fold_in(own, axis_at), (shards_of,), jnp.float32, smallest / len(split), largest / len(split)))
        level = level * jnp.repeat(steps, dims[axis_at] // shards_of).reshape([-1 if axis == axis_at else 1 for axis in range(len(dims))])
    return level


def split_up(number_of, total, reach, lean):
    portions = [(1 << 20) // math.isqrt(standing ** lean) + 1 for standing in range(2, number_of + 1)]
    rest, given = total - reach - (number_of - 1), [1] * (number_of - 1)
    while rest > 0:
        candidates = [i for i in range(number_of - 1) if given[i] < reach]
        whole, remaining = sum([portions[i] for i in candidates]), rest
        for i in candidates:
            extra = min(reach - given[i], max(1, remaining * portions[i] // whole), rest)
            given[i] = given[i] + extra
            rest = rest - extra
    return np.array([reach] + given)


def uneven(stream_key, number_of, total, reach, lean):
    if number_of == 2:
        one = jax.random.randint(stream_key, (), max(1, total - reach), min(reach, total - 1) + 1)
        return jnp.stack([one, total - one])
    sizes = jnp.asarray(split_up(number_of, total, reach, lean), jnp.int32)
    couples = (number_of - 1) // 2
    donor, sink = sizes[1:1 + 2 * couples:2], sizes[2:2 + 2 * couples:2]
    room = jnp.minimum(donor - 1, reach - sink)
    passed = jax.random.randint(jax.random.fold_in(stream_key, 1), (couples,), 0, 1 << 20) % (room + 1)
    sizes = sizes.at[1:1 + 2 * couples:2].set(donor - passed).at[2:2 + 2 * couples:2].set(sink + passed)
    return sizes[jax.random.permutation(jax.random.fold_in(stream_key, 2), number_of)]


def scatter_about(rng, dims, scale, most, pieces=(), kind=jnp.bfloat16):
    drawn = scale * jax.random.normal(rng, dims, jnp.float32)
    if pieces:
        drawn = drawn * block_scale(rng, dims, pieces, -0.22, 0.18)
    return jnp.clip(drawn, -most, most).astype(kind)


def setup_inputs(seed: int = 0) -> dict:
    arg_keys = jax.random.split(jax.random.key(seed), 14)
    corpus = scatter_about(arg_keys[0], (CORPUS, BLK, FEAT), 1.0, 6.0, ((0, 16),))
    picks = with_ends(jax.random.randint(arg_keys[1], (N_DP, N_DP), 0, CB), jax.random.fold_in(arg_keys[1], 1), 0, CB - 1).astype(jnp.int32)
    lengths = uneven(arg_keys[2], CORPUS, CORPUS * BLK * 3 // 4, BLK, 1).astype(jnp.int32)
    langs = with_ends(jax.random.randint(arg_keys[3], (CORPUS,), 0, LANGS), jax.random.fold_in(arg_keys[3], 1), 0, LANGS - 1).astype(jnp.int32)
    w_in = scatter_about(arg_keys[4], (FEAT, D), FEAT ** -0.5, 0.3125, ((1, 2),))
    lang_table = scatter_about(arg_keys[5], (LANGS, D), 0.5, 3.0, ((1, 2),))
    ln_gain = jnp.clip(1.0 + 0.18 * jax.random.normal(arg_keys[6], (D,), jnp.float32), 0.1, 1.9)
    w_pw1 = scatter_about(arg_keys[7], (D, 2, D), D ** -0.5, 0.15625, ((0, 16), (2, 2)))
    kernel = scatter_about(arg_keys[8], (KER, D), 0.3, 1.5, ((1, 2),), jnp.float32)
    bn_gain = jnp.clip(1.0 + 0.18 * jax.random.normal(arg_keys[9], (D,), jnp.float32), 0.1, 1.9)
    bn_bias = scatter_about(arg_keys[10], (D,), 0.5, 3.0, ((0, 2),), jnp.float32)
    w_pw2 = scatter_about(arg_keys[11], (D, D), D ** -0.5, 0.15625, ((0, 16), (1, 2)))
    cotangent = scatter_about(arg_keys[12], (TOTAL_ROWS, D), 1.0, 6.0, ((0, 16), (1, 2)))
    return {"corpus": corpus, "picks": picks, "lengths": lengths, "langs": langs, "w_in": w_in, "lang_table": lang_table, "ln_gain": ln_gain, "w_pw1": w_pw1, "kernel": kernel, "bn_gain": bn_gain, "bn_bias": bn_bias, "w_pw2": w_pw2, "cotangent": cotangent}


EPS = 1e-05

def depth_conv(values, taps):
    frames = BLK
    chans = values.shape[1]
    shaped = values.reshape(-1, frames, chans)
    margin = KER // 2
    padded = jnp.pad(shaped, ((0, 0), (margin, margin), (0, 0)))
    total = jnp.zeros(shaped.shape, jnp.float32)
    for step in range(KER):
        total = total + taps[step] * padded[:, step:step + frames]
    return total.reshape(values.shape)

def depth_back(grads, taps):
    frames = BLK
    chans = grads.shape[1]
    shaped = grads.reshape(-1, frames, chans)
    margin = KER // 2
    padded = jnp.pad(shaped, ((0, 0), (margin, margin), (0, 0)))
    total = jnp.zeros(shaped.shape, jnp.float32)
    for step in range(KER):
        begin = 2 * margin - step
        total = total + taps[step] * padded[:, begin:begin + frames]
    return total.reshape(grads.shape)

def kernel_terms(grads, values):
    frames = BLK
    chans = values.shape[1]
    shaped = values.reshape(-1, frames, chans)
    grad_shaped = grads.reshape(-1, frames, chans)
    margin = KER // 2
    padded = jnp.pad(shaped, ((0, 0), (margin, margin), (0, 0)))
    rows_out = []
    for step in range(KER):
        rows_out.append(lax.optimization_barrier(jnp.sum(grad_shaped * padded[:, step:step + frames], axis=(0, 1))))
    return jnp.stack(rows_out, 0)

def reference(corpus, picks, lengths, langs, w_in, lang_table, ln_gain, w_pw1, kernel, bn_gain, bn_bias, w_pw2, cotangent):
    block_ids = (jnp.arange(N_DP, dtype=jnp.int32)[None, :] * CB + picks.T).astype(jnp.int32).reshape(-1)
    chosen = corpus[block_ids]
    lens = lengths[block_ids]
    lang = langs[block_ids]
    valid = (jnp.arange(BLK, dtype=jnp.int32)[None, :] < lens[:, None]).astype(jnp.float32).reshape(-1)
    mel = chosen.reshape(-1, FEAT) * valid[:, None].astype(jnp.bfloat16)
    onehot = (lang[:, None] == jnp.arange(LANGS, dtype=jnp.int32)[None, :]).astype(jnp.bfloat16)
    lang_rows = jnp.dot(onehot, lang_table, preferred_element_type=jnp.float32)
    inputs = jnp.dot(mel, w_in, preferred_element_type=jnp.float32) + jnp.repeat(lang_rows, BLK, axis=0)
    mean = lax.optimization_barrier(jnp.sum(inputs, 1)) / D
    var = lax.optimization_barrier(jnp.sum(inputs * inputs, 1)) / D - mean * mean
    normed_in = ((inputs - mean[:, None]) * lax.rsqrt(var + EPS)[:, None] * ln_gain).astype(jnp.bfloat16)
    pre = jnp.dot(normed_in, w_pw1.reshape(D, 2 * D), preferred_element_type=jnp.float32)
    linear_part = pre[:, :D]
    gate_part = pre[:, D:]
    gate_sig = jax.nn.sigmoid(gate_part)
    glu_out = linear_part * gate_sig * valid[:, None]
    conv_out = depth_conv(glu_out, kernel)
    count = jnp.sum(valid)
    mu_conv = lax.optimization_barrier(jnp.sum(valid[:, None] * conv_out, 0)) / count
    var_conv = lax.optimization_barrier(jnp.sum(valid[:, None] * conv_out * conv_out, 0)) / count - mu_conv * mu_conv
    inv_std = lax.rsqrt(var_conv + EPS)
    normed_conv = (conv_out - mu_conv) * inv_std
    act = normed_conv * bn_gain + bn_bias
    act_sig = jax.nn.sigmoid(act)
    hidden = (valid[:, None] * act * act_sig).astype(jnp.bfloat16)
    encoded = (inputs + jnp.dot(hidden, w_pw2, preferred_element_type=jnp.float32)).astype(jnp.bfloat16)
    grad_pw2 = jnp.dot(hidden.T, cotangent, preferred_element_type=jnp.float32)
    dhidden = jnp.dot(cotangent, w_pw2.T, preferred_element_type=jnp.float32)
    dact = dhidden * valid[:, None] * act_sig * (1.0 + act * (1.0 - act_sig))
    grad_bias = lax.optimization_barrier(jnp.sum(dact, 0))
    grad_gain = lax.optimization_barrier(jnp.sum(dact * normed_conv, 0))
    dconv = valid[:, None] * inv_std * bn_gain * (dact - grad_bias / count - normed_conv * grad_gain / count)
    grad_kernel = kernel_terms(dconv, glu_out)
    dglu = depth_back(dconv, kernel)
    dlin = dglu * valid[:, None] * gate_sig
    dgate = dglu * valid[:, None] * linear_part * gate_sig * (1.0 - gate_sig)
    dpre = jnp.concatenate([dlin, dgate], 1).astype(jnp.bfloat16)
    grad_pw1 = jnp.dot(normed_in.T, dpre, preferred_element_type=jnp.float32).reshape(D, 2, D)
    return (encoded, grad_pw1, grad_pw2, grad_kernel, grad_gain, grad_bias)
```

```python
import functools

import jax
import jax.numpy as jnp
from jax import lax
from jax.experimental import pallas as pl
from jax.experimental.pallas import tpu as pltpu
from jax.sharding import PartitionSpec as P

EPS = 1e-05


def depth_conv(values, taps, frames):
    chans = values.shape[1]
    shaped = values.reshape(-1, frames, chans)
    margin = taps.shape[0] // 2
    padded = jnp.pad(shaped, ((0, 0), (margin, margin), (0, 0)))
    total = jnp.zeros(shaped.shape, jnp.float32)
    for step in range(taps.shape[0]):
        total = total + taps[step] * padded[:, step : step + frames]
    return total.reshape(values.shape)


def depth_back(grads, taps, frames):
    chans = grads.shape[1]
    shaped = grads.reshape(-1, frames, chans)
    margin = taps.shape[0] // 2
    padded = jnp.pad(shaped, ((0, 0), (margin, margin), (0, 0)))
    total = jnp.zeros(shaped.shape, jnp.float32)
    for step in range(taps.shape[0]):
        begin = 2 * margin - step
        total = total + taps[step] * padded[:, begin : begin + frames]
    return total.reshape(grads.shape)


def kernel_terms(grads, values, width, frames):
    chans = values.shape[1]
    shaped = values.reshape(-1, frames, chans)
    grad_shaped = grads.reshape(-1, frames, chans)
    margin = width // 2
    padded = jnp.pad(shaped, ((0, 0), (margin, margin), (0, 0)))
    rows_out = []
    for step in range(width):
        rows_out.append(jnp.sum(grad_shaped * padded[:, step : step + frames], axis=(0, 1)))
    return jnp.stack(rows_out, 0)


def contract_rows(left, right):
    return lax.dot_general(
        left, right, (((0,), (0,)), ((), ())), preferred_element_type=jnp.float32
    )


MESH = pl.DeviceIdType.MESH
F32 = jnp.float32
BF16 = jnp.bfloat16
VMEM = pl.BlockSpec(memory_space=pltpu.VMEM)
DMA = pltpu.SemaphoreType.DMA
LIMIT = 56 * 1024 * 1024


def greet(axes):
    barrier = pltpu.get_barrier_semaphore()
    total = 0
    for axis in axes:
        size, me = lax.axis_size(axis), lax.axis_index(axis)
        for k in range(1, size):
            pl.semaphore_signal(
                barrier, inc=1, device_id={axis: lax.rem(me + k, size)}, device_id_type=MESH
            )
        total += size - 1
    pl.semaphore_wait(barrier, total)


def push(src, dst, send, recv, axis, peer):
    copy = pltpu.make_async_remote_copy(
        src_ref=src,
        dst_ref=dst,
        send_sem=send,
        recv_sem=recv,
        device_id={axis: peer},
        device_id_type=MESH,
    )
    copy.start()
    return copy


def push_all(axis, source, slots, send, recv):
    size, me = lax.axis_size(axis), lax.axis_index(axis)
    copies = []
    for k in range(1, size):
        peer = lax.rem(me + k, size)
        copies.append(push(source(peer), slots.at[me], send.at[k], recv.at[k], axis, peer))
    return copies


def sum_slots(slots, size):
    total = slots[0]
    for p in range(1, size):
        total = total + slots[p]
    return total


def stats_kernel(x_ref, o_ref, slots, send, recv):
    size, me = lax.axis_size("dp"), lax.axis_index("dp")
    greet(("dp",))
    copies = push_all("dp", lambda peer: x_ref, slots, send, recv)
    slots[me] = x_ref[...]
    for copy in copies:
        copy.wait()
    o_ref[...] = sum_slots(slots, size)


def stats_sum(row, cid):
    n = lax.axis_size("dp")
    return pl.pallas_call(
        stats_kernel,
        out_shape=jax.ShapeDtypeStruct(row.shape, F32),
        in_specs=[VMEM],
        out_specs=VMEM,
        scratch_shapes=[pltpu.VMEM((n,) + row.shape, F32), DMA((n,)), DMA((n,))],
        compiler_params=pltpu.CompilerParams(collective_id=cid, has_side_effects=True),
        name="stats_sum",
    )(row)


def stats_hidden_kernel(
    x_ref, h_ref, o_ref, hid_ref, slots, hslots, send, recv, hsend, hrecv
):
    size, me = lax.axis_size("dp"), lax.axis_index("dp")
    parts, mine = lax.axis_size("mp"), lax.axis_index("mp")
    chans = h_ref.shape[1]
    greet(("dp", "mp"))
    copies = push_all("dp", lambda peer: x_ref, slots, send, recv)
    wide = push_all("mp", lambda peer: h_ref, hslots, hsend, hrecv)
    slots[me] = x_ref[...]
    hslots[mine] = h_ref[...]
    for copy in copies:
        copy.wait()
    o_ref[...] = sum_slots(slots, size)
    for copy in wide:
        copy.wait()
    for p in range(parts):
        hid_ref[:, p * chans : (p + 1) * chans] = hslots[p]


def stats_hidden(row, hidden, cid):
    n, q = lax.axis_size("dp"), lax.axis_size("mp")
    rows, chans = hidden.shape
    return pl.pallas_call(
        stats_hidden_kernel,
        out_shape=(
            jax.ShapeDtypeStruct(row.shape, F32),
            jax.ShapeDtypeStruct((rows, q * chans), BF16),
        ),
        in_specs=[VMEM, VMEM],
        out_specs=(VMEM, VMEM),
        scratch_shapes=[
            pltpu.VMEM((n,) + row.shape, F32),
            pltpu.VMEM((q,) + hidden.shape, BF16),
            DMA((n,)),
            DMA((n,)),
            DMA((q,)),
            DMA((q,)),
        ],
        compiler_params=pltpu.CompilerParams(
            collective_id=cid, has_side_effects=True, vmem_limit_bytes=LIMIT
        ),
        name="stats_hidden",
    )(row, hidden)


def grads_kernel(
    n,
    g1,
    g2,
    gk,
    o1,
    o2,
    ok,
    r1a,
    r1b,
    s1a,
    acc1,
    r2a,
    s2a,
    r3a,
    s1b,
    r2b,
    acc2,
    s2b,
    r3b,
    kslots,
    ksum,
    kall,
    core_sem,
    xa_sem,
    za_sem,
    zb_sem,
    xb_sem,
    k_sem,
    k2_sem,
):
    m = n // 4
    me = lax.axis_index("dp")
    c = lax.rem(me, 2)
    b = lax.rem(me // 2, 2)
    a = me // 4
    core_peer = me + 1 - 2 * c
    x_peer = me + 2 - 4 * b
    greet(("dp",))

    copy_1a = push(g1.at[:, :, 1 - c], r1a, core_sem.at[0, 0], core_sem.at[1, 0], "dp", core_peer)
    copy_1b = push(g2.at[:, :, 1 - c], r1b, core_sem.at[0, 1], core_sem.at[1, 1], "dp", core_peer)
    k_copies = push_all("dp", lambda peer: gk.at[peer], kslots, k_sem.at[0], k_sem.at[1])
    kslots[me] = gk[me]

    order = [lax.rem(a + k, m) for k in range(m)]
    steps = list(range(1, m)) + [0]

    copy_1a.wait_recv()
    xa = {}
    for k in steps:
        to = order[k]
        s1a[to] = (
            g1[to, 1 - b, c].astype(F32) + r1a[to, 1 - b].astype(F32)
        ).astype(BF16)
        xa[k] = push(s1a.at[to], r2a.at[to], xa_sem.at[0, k], xa_sem.at[1, k], "dp", x_peer)
    copy_1b.wait_recv()
    zb = []
    for k in steps:
        to = order[k]
        if k == 0:
            for j in range(2):
                acc2[j] = g2[to, j, c].astype(F32) + r1b[to, j].astype(F32)
            continue
        for j in range(2):
            s1b[to, j] = (g2[to, j, c].astype(F32) + r1b[to, j].astype(F32)).astype(BF16)
        peer = to * 4 + b * 2 + c
        zb.append(push(s1b.at[to], r2b.at[a], zb_sem.at[0, k], zb_sem.at[1, k], "dp", peer))
    for k in steps:
        to = order[k]
        acc1[to] = g1[to, b, c].astype(F32) + r1a[to, b].astype(F32)

    for copy in k_copies:
        copy.wait()
    ksum[...] = sum_slots(kslots, n)
    k2_copies = push_all("dp", lambda peer: ksum, kall, k2_sem.at[0], k2_sem.at[1])
    kall[me] = ksum[...]

    za = []
    for k in steps:
        to = order[k]
        xa[k].wait()
        if k == 0:
            continue
        s2a[to] = (acc1[to] + r2a[to].astype(F32)).astype(BF16)
        peer = to * 4 + b * 2 + c
        za.append(push(s2a.at[to], r3a.at[a], za_sem.at[0, k], za_sem.at[1, k], "dp", peer))

    for copy in zb:
        copy.wait()
    for k in range(1, m):
        frm = lax.rem(a - k + m, m)
        for j in range(2):
            acc2[j] = acc2[j] + r2b[frm, j].astype(F32)
    s2b[...] = acc2[1 - b].astype(BF16)
    xb = push(s2b, r3b, xb_sem.at[0], xb_sem.at[1], "dp", x_peer)

    o1[...] = acc1[a] + r2a[a].astype(F32)
    for copy in k2_copies:
        copy.wait()
    ok[...] = kall[...]
    xb.wait()
    o2[...] = acc2[b] + r3b[...].astype(F32)
    for copy in za:
        copy.wait()
    total = o1[...]
    for k in range(1, m):
        total = total + r3a[lax.rem(a - k + m, m)].astype(F32)
    o1[...] = total
    copy_1a.wait_send()
    copy_1b.wait_send()


def grads_sum(g1, g2, gk, cid):
    n = lax.axis_size("dp")
    m = n // 4
    rows, wide = g1.shape[0] // n, g1.shape[1]
    chans = g2.shape[1]
    flat = gk.reshape(-1)
    part = -(-flat.shape[0] // (n * 128)) * 128
    flat = jnp.pad(flat, (0, n * part - flat.shape[0])).reshape(n, 1, part)
    o1, o2, ok = pl.pallas_call(
        functools.partial(grads_kernel, n),
        out_shape=(
            jax.ShapeDtypeStruct((rows, wide), F32),
            jax.ShapeDtypeStruct((rows, chans), F32),
            jax.ShapeDtypeStruct((n, 1, part), F32),
        ),
        in_specs=[VMEM] * 3,
        out_specs=(VMEM,) * 3,
        scratch_shapes=[
            pltpu.VMEM((m, 2, rows, wide), BF16),
            pltpu.VMEM((m, 2, rows, chans), BF16),
            pltpu.VMEM((m, rows, wide), BF16),
            pltpu.VMEM((m, rows, wide), F32),
            pltpu.VMEM((m, rows, wide), BF16),
            pltpu.VMEM((m, rows, wide), BF16),
            pltpu.VMEM((m, rows, wide), BF16),
            pltpu.VMEM((m, 2, rows, chans), BF16),
            pltpu.VMEM((m, 2, rows, chans), BF16),
            pltpu.VMEM((2, rows, chans), F32),
            pltpu.VMEM((rows, chans), BF16),
            pltpu.VMEM((rows, chans), BF16),
            pltpu.VMEM((n, 1, part), F32),
            pltpu.VMEM((1, part), F32),
            pltpu.VMEM((n, 1, part), F32),
            DMA((2, 2)),
            DMA((2, m)),
            DMA((2, m)),
            DMA((2, m)),
            DMA((2,)),
            DMA((2, n)),
            DMA((2, n)),
        ],
        compiler_params=pltpu.CompilerParams(
            collective_id=cid, has_side_effects=True, vmem_limit_bytes=LIMIT
        ),
        name="grads_sum",
    )(
        g1.reshape(m, 2, 2, rows, wide),
        g2.reshape(m, 2, 2, rows, chans),
        flat,
    )
    return o1, o2, ok.reshape(-1)[: gk.size].reshape(gk.shape)


def on_device(
    corpus,
    picks,
    lengths,
    langs,
    w_in,
    lang_table,
    ln_gain,
    w_pw1,
    kernel,
    bn_gain,
    bn_bias,
    w_pw2,
    cotangent,
):
    model_width = w_pw2.shape[0] * lax.axis_size("dp")
    parts = lax.axis_size("mp")
    weights_one = lax.all_gather(w_pw1, "dp", axis=0, tiled=True).reshape(model_width, -1)
    half = weights_one.shape[1] // 2
    feats = corpus.shape[2]
    frames = corpus.shape[1]
    picked = picks[0][:, None] == jnp.arange(corpus.shape[0], dtype=jnp.int32)[None, :]
    blocks = jnp.einsum(
        "sb,bfk->sfk", picked.astype(BF16), corpus, preferred_element_type=F32
    ).astype(BF16)
    lens_send = jnp.sum(jnp.where(picked, lengths[None, :], 0), 1)
    lang_send = jnp.sum(jnp.where(picked, langs[None, :], 0), 1)
    whole = jnp.stack([lens_send, lang_send], 1).astype(BF16)
    whole = jnp.broadcast_to(whole[:, None, :], (whole.shape[0], frames, 2))
    packed = jnp.concatenate([blocks, whole], 2)
    received = lax.all_to_all(packed, "dp", split_axis=0, concat_axis=0, tiled=True)
    lens = received[:, 0, feats].astype(jnp.int32)
    lang = received[:, 0, feats + 1].astype(jnp.int32)
    valid = (
        (jnp.arange(frames, dtype=jnp.int32)[None, :] < lens[:, None]).astype(F32).reshape(-1)
    )
    valid_col = valid[:, None]
    mel = received[:, :, :feats].reshape(-1, feats) * valid_col.astype(BF16)
    onehot = (lang[:, None] == jnp.arange(lang_table.shape[0], dtype=jnp.int32)[None, :]).astype(
        BF16
    )
    onehot = jnp.repeat(onehot, frames, axis=0)
    left = jnp.concatenate([mel, onehot], 1)
    right = jnp.concatenate([w_in, lang_table], 0)
    right_full = lax.all_gather(right, "mp", axis=1, tiled=True)
    gain_full = lax.all_gather(ln_gain, "mp", axis=0, tiled=True)
    inputs = jnp.dot(left, right, preferred_element_type=F32)
    full_in = jnp.dot(left, right_full, preferred_element_type=F32)
    mean = jnp.sum(full_in, 1) / model_width
    var = jnp.sum(full_in * full_in, 1) / model_width - mean * mean
    normed_full = (
        (full_in - mean[:, None]) * lax.rsqrt(var + EPS)[:, None] * gain_full
    ).astype(BF16)
    pre = jnp.dot(normed_full, weights_one, preferred_element_type=jnp.float32)
    linear_part = pre[:, :half]
    gate_part = pre[:, half:]
    gate_sig = jax.nn.sigmoid(gate_part)
    glu_out = linear_part * gate_sig * valid_col
    conv_out = depth_conv(glu_out, kernel, frames)
    row = jnp.concatenate(
        [
            jnp.sum(valid_col * conv_out, 0),
            jnp.sum(valid_col * conv_out * conv_out, 0),
            jnp.full((128,), jnp.sum(valid), F32),
        ]
    )[None]
    row = stats_sum(row, 1)
    sum_conv, sum_sq, count = row[0, :half], row[0, half : 2 * half], row[0, 2 * half]
    mu_conv = sum_conv / count
    var_conv = sum_sq / count - mu_conv * mu_conv
    inv_std = lax.rsqrt(var_conv + EPS)
    normed_conv = (conv_out - mu_conv) * inv_std
    act = normed_conv * bn_gain + bn_bias
    act_sig = jax.nn.sigmoid(act)
    hidden = (valid_col * act * act_sig).astype(jnp.bfloat16)
    w_later, _ = lax.optimization_barrier((w_pw2, weights_one))
    weights_two = lax.all_gather(w_later, "dp", axis=0, tiled=True)
    partial = lax.dot_general(
        cotangent, weights_two, (((1,), (1,)), ((), ())), preferred_element_type=F32
    ).astype(BF16)
    partial = jnp.stack([partial[:, p * half : (p + 1) * half] for p in range(parts)], 0)
    partial = lax.all_to_all(partial, "mp", split_axis=0, concat_axis=0, tiled=True)
    dhidden = jnp.sum(partial.astype(F32), 0)
    dact = dhidden * valid_col * act_sig * (1.0 + act * (1.0 - act_sig))
    row2 = jnp.concatenate([jnp.sum(dact, 0), jnp.sum(dact * normed_conv, 0)])[None]
    row2, hidden_full = stats_hidden(row2, hidden, 2)
    grad_bias, grad_gain = row2[0, :half], row2[0, half:]
    encoded = (inputs + jnp.dot(hidden_full, weights_two, preferred_element_type=F32)).astype(
        BF16
    )
    part_pw2 = contract_rows(hidden_full, cotangent).astype(BF16)
    dconv = (
        valid_col * inv_std * bn_gain * (dact - grad_bias / count - normed_conv * grad_gain / count)
    )
    part_kernel = kernel_terms(dconv, glu_out, kernel.shape[0], frames)
    dglu = depth_back(dconv, kernel, frames)
    dlin = dglu * valid_col * gate_sig
    dgate = dglu * valid_col * linear_part * gate_sig * (1.0 - gate_sig)
    dpre = jnp.concatenate([dlin, dgate], 1).astype(jnp.bfloat16)
    part_pw1 = contract_rows(normed_full, dpre).astype(BF16)
    grad_pw1, grad_pw2, grad_kernel = grads_sum(part_pw1, part_pw2, part_kernel, 3)
    grad_pw1 = grad_pw1.reshape(grad_pw1.shape[0], 2, half)
    return (encoded, grad_pw1, grad_pw2, grad_kernel, grad_gain, grad_bias)


def solution(mesh):
    return jax.shard_map(
        on_device,
        mesh=mesh,
        in_specs=(
            P("dp", None, None),
            P("dp", None),
            P("dp"),
            P("dp"),
            P(None, "mp"),
            P(None, "mp"),
            P("mp"),
            P("dp", None, "mp"),
            P(None, "mp"),
            P("mp"),
            P("mp"),
            P("dp", "mp"),
            P("dp", "mp"),
        ),
        out_specs=(
            P("dp", "mp"),
            P("dp", None, "mp"),
            P("dp", "mp"),
            P(None, "mp"),
            P("mp"),
            P("mp"),
        ),
        check_vma=False,
    )
```

```python
import functools

import jax
import jax.numpy as jnp
from jax import lax
from jax.experimental import pallas as pl
from jax.experimental.pallas import tpu as pltpu
from jax.sharding import PartitionSpec as P

EPS = 1e-05


def depth_conv(values, taps, frames):
    chans = values.shape[1]
    shaped = values.reshape(-1, frames, chans)
    margin = taps.shape[0] // 2
    padded = jnp.pad(shaped, ((0, 0), (margin, margin), (0, 0)))
    total = jnp.zeros(shaped.shape, jnp.float32)
    for step in range(taps.shape[0]):
        total = total + taps[step] * padded[:, step : step + frames]
    return total.reshape(values.shape)


def depth_back(grads, taps, frames):
    chans = grads.shape[1]
    shaped = grads.reshape(-1, frames, chans)
    margin = taps.shape[0] // 2
    padded = jnp.pad(shaped, ((0, 0), (margin, margin), (0, 0)))
    total = jnp.zeros(shaped.shape, jnp.float32)
    for step in range(taps.shape[0]):
        begin = 2 * margin - step
        total = total + taps[step] * padded[:, begin : begin + frames]
    return total.reshape(grads.shape)


def kernel_terms(grads, values, width, frames):
    chans = values.shape[1]
    shaped = values.reshape(-1, frames, chans)
    grad_shaped = grads.reshape(-1, frames, chans)
    margin = width // 2
    padded = jnp.pad(shaped, ((0, 0), (margin, margin), (0, 0)))
    rows_out = []
    for step in range(width):
        rows_out.append(jnp.sum(grad_shaped * padded[:, step : step + frames], axis=(0, 1)))
    return jnp.stack(rows_out, 0)


def contract_rows(left, right):
    return lax.dot_general(
        left, right, (((0,), (0,)), ((), ())), preferred_element_type=jnp.float32
    )


MESH = pl.DeviceIdType.MESH
F32 = jnp.float32
BF16 = jnp.bfloat16
VMEM = pl.BlockSpec(memory_space=pltpu.VMEM)
DMA = pltpu.SemaphoreType.DMA
LIMIT = 56 * 1024 * 1024


def greet(axes):
    barrier = pltpu.get_barrier_semaphore()
    total = 0
    for axis in axes:
        size, me = lax.axis_size(axis), lax.axis_index(axis)
        for k in range(1, size):
            pl.semaphore_signal(
                barrier, inc=1, device_id={axis: lax.rem(me + k, size)}, device_id_type=MESH
            )
        total += size - 1
    pl.semaphore_wait(barrier, total)


def push(src, dst, send, recv, axis, peer):
    copy = pltpu.make_async_remote_copy(
        src_ref=src,
        dst_ref=dst,
        send_sem=send,
        recv_sem=recv,
        device_id={axis: peer},
        device_id_type=MESH,
    )
    copy.start()
    return copy


def push_all(axis, source, slots, send, recv):
    size, me = lax.axis_size(axis), lax.axis_index(axis)
    copies = []
    for k in range(1, size):
        peer = lax.rem(me + k, size)
        copies.append(push(source(peer), slots.at[me], send.at[k], recv.at[k], axis, peer))
    return copies


def sum_slots(slots, size):
    total = slots[0]
    for p in range(1, size):
        total = total + slots[p]
    return total


def stats_kernel(x_ref, o_ref, slots, send, recv):
    size, me = lax.axis_size("dp"), lax.axis_index("dp")
    greet(("dp",))
    copies = push_all("dp", lambda peer: x_ref, slots, send, recv)
    slots[me] = x_ref[...]
    for copy in copies:
        copy.wait()
    o_ref[...] = sum_slots(slots, size)


def stats_sum(row, cid):
    n = lax.axis_size("dp")
    return pl.pallas_call(
        stats_kernel,
        out_shape=jax.ShapeDtypeStruct(row.shape, F32),
        in_specs=[VMEM],
        out_specs=VMEM,
        scratch_shapes=[pltpu.VMEM((n,) + row.shape, F32), DMA((n,)), DMA((n,))],
        compiler_params=pltpu.CompilerParams(collective_id=cid, has_side_effects=True),
        name="stats_sum",
    )(row)


def stats_hidden_kernel(
    x_ref, h_ref, o_ref, hid_ref, slots, hslots, send, recv, hsend, hrecv
):
    size, me = lax.axis_size("dp"), lax.axis_index("dp")
    parts, mine = lax.axis_size("mp"), lax.axis_index("mp")
    chans = h_ref.shape[1]
    greet(("dp", "mp"))
    copies = push_all("dp", lambda peer: x_ref, slots, send, recv)
    wide = push_all("mp", lambda peer: h_ref, hslots, hsend, hrecv)
    slots[me] = x_ref[...]
    hslots[mine] = h_ref[...]
    for copy in copies:
        copy.wait()
    o_ref[...] = sum_slots(slots, size)
    for copy in wide:
        copy.wait()
    for p in range(parts):
        hid_ref[:, p * chans : (p + 1) * chans] = hslots[p]


def stats_hidden(row, hidden, cid):
    n, q = lax.axis_size("dp"), lax.axis_size("mp")
    rows, chans = hidden.shape
    return pl.pallas_call(
        stats_hidden_kernel,
        out_shape=(
            jax.ShapeDtypeStruct(row.shape, F32),
            jax.ShapeDtypeStruct((rows, q * chans), BF16),
        ),
        in_specs=[VMEM, VMEM],
        out_specs=(VMEM, VMEM),
        scratch_shapes=[
            pltpu.VMEM((n,) + row.shape, F32),
            pltpu.VMEM((q,) + hidden.shape, BF16),
            DMA((n,)),
            DMA((n,)),
            DMA((q,)),
            DMA((q,)),
        ],
        compiler_params=pltpu.CompilerParams(
            collective_id=cid, has_side_effects=True, vmem_limit_bytes=LIMIT
        ),
        name="stats_hidden",
    )(row, hidden)


def grads_kernel(
    n,
    g1,
    g2,
    gk,
    o1,
    o2,
    ok,
    r1a,
    r1b,
    s1a,
    acc1,
    r2a,
    s2a,
    r3a,
    s1b,
    r2b,
    acc2,
    s2b,
    r3b,
    kslots,
    ksum,
    kall,
    core_sem,
    xa_sem,
    za_sem,
    zb_sem,
    xb_sem,
    k_sem,
    k2_sem,
):
    m = n // 4
    me = lax.axis_index("dp")
    c = lax.rem(me, 2)
    b = lax.rem(me // 2, 2)
    a = me // 4
    core_peer = me + 1 - 2 * c
    x_peer = me + 2 - 4 * b
    greet(("dp",))

    copy_1a = push(g1.at[:, :, 1 - c], r1a, core_sem.at[0, 0], core_sem.at[1, 0], "dp", core_peer)
    copy_1b = push(g2.at[:, :, 1 - c], r1b, core_sem.at[0, 1], core_sem.at[1, 1], "dp", core_peer)
    k_copies = push_all("dp", lambda peer: gk.at[peer], kslots, k_sem.at[0], k_sem.at[1])
    kslots[me] = gk[me]

    order = [lax.rem(a + k, m) for k in range(m)]
    steps = list(range(1, m)) + [0]

    copy_1a.wait_recv()
    xa = {}
    for k in steps:
        to = order[k]
        s1a[to] = (
            g1[to, 1 - b, c].astype(F32) + r1a[to, 1 - b].astype(F32)
        ).astype(BF16)
        xa[k] = push(s1a.at[to], r2a.at[to], xa_sem.at[0, k], xa_sem.at[1, k], "dp", x_peer)
    copy_1b.wait_recv()
    zb = []
    for k in steps:
        to = order[k]
        if k == 0:
            for j in range(2):
                acc2[j] = g2[to, j, c].astype(F32) + r1b[to, j].astype(F32)
            continue
        for j in range(2):
            s1b[to, j] = (g2[to, j, c].astype(F32) + r1b[to, j].astype(F32)).astype(BF16)
        peer = to * 4 + b * 2 + c
        zb.append(push(s1b.at[to], r2b.at[a], zb_sem.at[0, k], zb_sem.at[1, k], "dp", peer))
    for k in steps:
        to = order[k]
        acc1[to] = g1[to, b, c].astype(F32) + r1a[to, b].astype(F32)

    for copy in k_copies:
        copy.wait()
    ksum[...] = sum_slots(kslots, n)
    k2_copies = push_all("dp", lambda peer: ksum, kall, k2_sem.at[0], k2_sem.at[1])
    kall[me] = ksum[...]

    za = []
    for k in steps:
        to = order[k]
        xa[k].wait()
        if k == 0:
            continue
        s2a[to] = (acc1[to] + r2a[to].astype(F32)).astype(BF16)
        peer = to * 4 + b * 2 + c
        za.append(push(s2a.at[to], r3a.at[a], za_sem.at[0, k], za_sem.at[1, k], "dp", peer))

    for copy in zb:
        copy.wait()
    for k in range(1, m):
        frm = lax.rem(a - k + m, m)
        for j in range(2):
            acc2[j] = acc2[j] + r2b[frm, j].astype(F32)
    s2b[...] = acc2[1 - b].astype(BF16)
    xb = push(s2b, r3b, xb_sem.at[0], xb_sem.at[1], "dp", x_peer)

    o1[...] = acc1[a] + r2a[a].astype(F32)
    for copy in k2_copies:
        copy.wait()
    ok[...] = kall[...]
    xb.wait()
    o2[...] = acc2[b] + r3b[...].astype(F32)
    for copy in za:
        copy.wait()
    total = o1[...]
    for k in range(1, m):
        total = total + r3a[lax.rem(a - k + m, m)].astype(F32)
    o1[...] = total
    copy_1a.wait_send()
    copy_1b.wait_send()


def grads_sum(g1, g2, gk, cid):
    n = lax.axis_size("dp")
    m = n // 4
    rows, wide = g1.shape[0] // n, g1.shape[1]
    chans = g2.shape[1]
    flat = gk.reshape(-1)
    part = -(-flat.shape[0] // (n * 128)) * 128
    flat = jnp.pad(flat, (0, n * part - flat.shape[0])).reshape(n, 1, part)
    o1, o2, ok = pl.pallas_call(
        functools.partial(grads_kernel, n),
        out_shape=(
            jax.ShapeDtypeStruct((rows, wide), F32),
            jax.ShapeDtypeStruct((rows, chans), F32),
            jax.ShapeDtypeStruct((n, 1, part), F32),
        ),
        in_specs=[VMEM] * 3,
        out_specs=(VMEM,) * 3,
        scratch_shapes=[
            pltpu.VMEM((m, 2, rows, wide), BF16),
            pltpu.VMEM((m, 2, rows, chans), BF16),
            pltpu.VMEM((m, rows, wide), BF16),
            pltpu.VMEM((m, rows, wide), F32),
            pltpu.VMEM((m, rows, wide), BF16),
            pltpu.VMEM((m, rows, wide), BF16),
            pltpu.VMEM((m, rows, wide), BF16),
            pltpu.VMEM((m, 2, rows, chans), BF16),
            pltpu.VMEM((m, 2, rows, chans), BF16),
            pltpu.VMEM((2, rows, chans), F32),
            pltpu.VMEM((rows, chans), BF16),
            pltpu.VMEM((rows, chans), BF16),
            pltpu.VMEM((n, 1, part), F32),
            pltpu.VMEM((1, part), F32),
            pltpu.VMEM((n, 1, part), F32),
            DMA((2, 2)),
            DMA((2, m)),
            DMA((2, m)),
            DMA((2, m)),
            DMA((2,)),
            DMA((2, n)),
            DMA((2, n)),
        ],
        compiler_params=pltpu.CompilerParams(
            collective_id=cid, has_side_effects=True, vmem_limit_bytes=LIMIT
        ),
        name="grads_sum",
    )(
        g1.reshape(m, 2, 2, rows, wide),
        g2.reshape(m, 2, 2, rows, chans),
        flat,
    )
    return o1, o2, ok.reshape(-1)[: gk.size].reshape(gk.shape)


def spread_kernel(
    n, w1, w2, pk, rt, gn, f1, f2, rec, rts, gns, z_sem, x_sem, core_sem, p_sem, r_sem, g_sem
):
    m = n // 4
    me, mine = lax.axis_index("dp"), lax.axis_index("mp")
    c = lax.rem(me, 2)
    b = lax.rem(me // 2, 2)
    a = me // 4
    core_peer = me + 1 - 2 * c
    x_peer = me + 2 - 4 * b
    greet(("dp", "mp"))
    small = push_all("dp", lambda peer: pk.at[peer], rec, p_sem.at[0], p_sem.at[1])
    full = (f1, f2)
    z, x, core = ({}, {}), ({}, {}), ({}, {})

    def to_core(i, src, at, j):
        core[i][j] = push(
            src, full[i].at[at], core_sem.at[i, 0, j], core_sem.at[i, 1, j], "dp", core_peer
        )

    def to_x(i, src, at, k):
        x[i][k] = push(src, full[i].at[at], x_sem.at[i, 0, k], x_sem.at[i, 1, k], "dp", x_peer)

    for i, w in enumerate((w1, w2)):
        for k in range(1, m):
            peer = lax.rem(a + k, m) * 4 + b * 2 + c
            z[i][k] = push(w, full[i].at[me], z_sem.at[i, 0, k], z_sem.at[i, 1, k], "dp", peer)
        to_x(i, w, me, 0)
        to_core(i, w, me, 0)
    small += push_all("mp", lambda peer: rt, rts, r_sem.at[0], r_sem.at[1])
    small += push_all("mp", lambda peer: gn, gns, g_sem.at[0], g_sem.at[1])
    f1[me] = w1[...]
    f2[me] = w2[...]
    rec[me] = pk[me]
    rts[mine] = rt[...]
    gns[mine] = gn[...]

    def z_step(i, k):
        z[i][k].wait_recv()
        at = lax.rem(a - k + m, m) * 4 + b * 2 + c
        to_x(i, full[i].at[at], at, k)
        to_core(i, full[i].at[at], at, k)

    def x_step(i, k):
        x[i][k].wait_recv()
        at = lax.rem(a - k + m, m) * 4 + (1 - b) * 2 + c
        to_core(i, full[i].at[at], at, m + k)

    for k in range(1, m):
        z_step(0, k)
    x_step(0, 0)
    for k in range(1, m):
        z_step(1, k)
        x_step(0, k)
    for k in range(m):
        x_step(1, k)
    for copy in small:
        copy.wait()
    for i in range(2):
        for copy in z[i].values():
            copy.wait_send()
        for copy in x[i].values():
            copy.wait_send()
        for copy in core[i].values():
            copy.wait()


def spread(w1, w2, packed, right, gain, cid):
    n, q = lax.axis_size("dp"), lax.axis_size("mp")
    m = n // 4
    return pl.pallas_call(
        functools.partial(spread_kernel, n),
        out_shape=(
            jax.ShapeDtypeStruct((n,) + w1.shape, BF16),
            jax.ShapeDtypeStruct((n,) + w2.shape, BF16),
            jax.ShapeDtypeStruct(packed.shape, BF16),
            jax.ShapeDtypeStruct((q,) + right.shape, BF16),
            jax.ShapeDtypeStruct((q,) + gain.shape, F32),
        ),
        in_specs=[VMEM] * 5,
        out_specs=(VMEM,) * 5,
        scratch_shapes=[
            DMA((2, 2, m)),
            DMA((2, 2, m)),
            DMA((2, 2, 2 * m)),
            DMA((2, n)),
            DMA((2, q)),
            DMA((2, q)),
        ],
        compiler_params=pltpu.CompilerParams(
            collective_id=cid, has_side_effects=True, vmem_limit_bytes=LIMIT
        ),
        name="spread",
    )(w1, w2, packed, right, gain)


def on_device(
    corpus,
    picks,
    lengths,
    langs,
    w_in,
    lang_table,
    ln_gain,
    w_pw1,
    kernel,
    bn_gain,
    bn_bias,
    w_pw2,
    cotangent,
):
    model_width = w_pw2.shape[0] * lax.axis_size("dp")
    parts = lax.axis_size("mp")
    half = w_pw2.shape[1]
    feats = corpus.shape[2]
    frames = corpus.shape[1]
    picked = picks[0][:, None] == jnp.arange(corpus.shape[0], dtype=jnp.int32)[None, :]
    blocks = jnp.einsum(
        "sb,bfk->sfk", picked.astype(BF16), corpus, preferred_element_type=F32
    ).astype(BF16)
    lens_send = jnp.sum(jnp.where(picked, lengths[None, :], 0), 1)
    lang_send = jnp.sum(jnp.where(picked, langs[None, :], 0), 1)
    whole = jnp.stack([lens_send, lang_send], 1).astype(BF16)
    whole = jnp.broadcast_to(whole[:, None, :], (whole.shape[0], frames, 2))
    lanes = -(-(feats + 2) // 128) * 128
    spare = jnp.zeros((whole.shape[0], frames, lanes - feats - 2), BF16)
    packed = jnp.concatenate([blocks, whole, spare], 2)
    right = jnp.concatenate([w_in, lang_table], 0)
    weights_one, weights_two, received, right_full, gain_full = spread(
        w_pw1.reshape(w_pw1.shape[0], -1), w_pw2, packed, right, ln_gain[None], 4
    )
    weights_one = weights_one.reshape(model_width, -1)
    weights_two = weights_two.reshape(model_width, -1)
    lens = received[:, 0, feats].astype(jnp.int32)
    lang = received[:, 0, feats + 1].astype(jnp.int32)
    valid = (
        (jnp.arange(frames, dtype=jnp.int32)[None, :] < lens[:, None]).astype(F32).reshape(-1)
    )
    valid_col = valid[:, None]
    mel = received[:, :, :feats].reshape(-1, feats) * valid_col.astype(BF16)
    onehot = (lang[:, None] == jnp.arange(lang_table.shape[0], dtype=jnp.int32)[None, :]).astype(
        BF16
    )
    onehot = jnp.repeat(onehot, frames, axis=0)
    left = jnp.concatenate([mel, onehot], 1)
    inputs = jnp.dot(left, right, preferred_element_type=F32)
    full_in = jnp.concatenate(
        [jnp.dot(left, right_full[p], preferred_element_type=F32) for p in range(parts)], 1
    )
    gain_full = gain_full.reshape(-1)
    mean = jnp.sum(full_in, 1) / model_width
    var = jnp.sum(full_in * full_in, 1) / model_width - mean * mean
    normed_full = (
        (full_in - mean[:, None]) * lax.rsqrt(var + EPS)[:, None] * gain_full
    ).astype(BF16)
    pre = jnp.dot(normed_full, weights_one, preferred_element_type=jnp.float32)
    linear_part = pre[:, :half]
    gate_part = pre[:, half:]
    gate_sig = jax.nn.sigmoid(gate_part)
    glu_out = linear_part * gate_sig * valid_col
    conv_out = depth_conv(glu_out, kernel, frames)
    row = jnp.concatenate(
        [
            jnp.sum(valid_col * conv_out, 0),
            jnp.sum(valid_col * conv_out * conv_out, 0),
            jnp.full((128,), jnp.sum(valid), F32),
        ]
    )[None]
    row = stats_sum(row, 1)
    sum_conv, sum_sq, count = row[0, :half], row[0, half : 2 * half], row[0, 2 * half]
    mu_conv = sum_conv / count
    var_conv = sum_sq / count - mu_conv * mu_conv
    inv_std = lax.rsqrt(var_conv + EPS)
    normed_conv = (conv_out - mu_conv) * inv_std
    act = normed_conv * bn_gain + bn_bias
    act_sig = jax.nn.sigmoid(act)
    hidden = (valid_col * act * act_sig).astype(jnp.bfloat16)
    partial = lax.dot_general(
        cotangent, weights_two, (((1,), (1,)), ((), ())), preferred_element_type=F32
    ).astype(BF16)
    partial = jnp.stack([partial[:, p * half : (p + 1) * half] for p in range(parts)], 0)
    partial = lax.all_to_all(partial, "mp", split_axis=0, concat_axis=0, tiled=True)
    dhidden = jnp.sum(partial.astype(F32), 0)
    dact = dhidden * valid_col * act_sig * (1.0 + act * (1.0 - act_sig))
    row2 = jnp.concatenate([jnp.sum(dact, 0), jnp.sum(dact * normed_conv, 0)])[None]
    row2, hidden_full = stats_hidden(row2, hidden, 2)
    grad_bias, grad_gain = row2[0, :half], row2[0, half:]
    encoded = (inputs + jnp.dot(hidden_full, weights_two, preferred_element_type=F32)).astype(
        BF16
    )
    part_pw2 = contract_rows(hidden_full, cotangent).astype(BF16)
    dconv = (
        valid_col * inv_std * bn_gain * (dact - grad_bias / count - normed_conv * grad_gain / count)
    )
    part_kernel = kernel_terms(dconv, glu_out, kernel.shape[0], frames)
    dglu = depth_back(dconv, kernel, frames)
    dlin = dglu * valid_col * gate_sig
    dgate = dglu * valid_col * linear_part * gate_sig * (1.0 - gate_sig)
    dpre = jnp.concatenate([dlin, dgate], 1).astype(jnp.bfloat16)
    part_pw1 = contract_rows(normed_full, dpre).astype(BF16)
    grad_pw1, grad_pw2, grad_kernel = grads_sum(part_pw1, part_pw2, part_kernel, 3)
    grad_pw1 = grad_pw1.reshape(grad_pw1.shape[0], 2, half)
    return (encoded, grad_pw1, grad_pw2, grad_kernel, grad_gain, grad_bias)


def solution(mesh):
    return jax.shard_map(
        on_device,
        mesh=mesh,
        in_specs=(
            P("dp", None, None),
            P("dp", None),
            P("dp"),
            P("dp"),
            P(None, "mp"),
            P(None, "mp"),
            P("mp"),
            P("dp", None, "mp"),
            P(None, "mp"),
            P("mp"),
            P("mp"),
            P("dp", "mp"),
            P("dp", "mp"),
        ),
        out_specs=(
            P("dp", "mp"),
            P("dp", None, "mp"),
            P("dp", "mp"),
            P(None, "mp"),
            P("mp"),
            P("mp"),
        ),
        check_vma=False,
    )
```

```python
import functools

import jax
import jax.numpy as jnp
from jax import lax
from jax.experimental import pallas as pl
from jax.experimental.pallas import tpu as pltpu
from jax.sharding import PartitionSpec as P

EPS = 1e-05


def depth_conv(values, taps, frames):
    chans = values.shape[1]
    shaped = values.reshape(-1, frames, chans)
    margin = taps.shape[0] // 2
    padded = jnp.pad(shaped, ((0, 0), (margin, margin), (0, 0)))
    total = jnp.zeros(shaped.shape, jnp.float32)
    for step in range(taps.shape[0]):
        total = total + taps[step] * padded[:, step : step + frames]
    return total.reshape(values.shape)


def depth_back(grads, taps, frames):
    chans = grads.shape[1]
    shaped = grads.reshape(-1, frames, chans)
    margin = taps.shape[0] // 2
    padded = jnp.pad(shaped, ((0, 0), (margin, margin), (0, 0)))
    total = jnp.zeros(shaped.shape, jnp.float32)
    for step in range(taps.shape[0]):
        begin = 2 * margin - step
        total = total + taps[step] * padded[:, begin : begin + frames]
    return total.reshape(grads.shape)


def kernel_terms(grads, values, width, frames):
    chans = values.shape[1]
    shaped = values.reshape(-1, frames, chans)
    grad_shaped = grads.reshape(-1, frames, chans)
    margin = width // 2
    padded = jnp.pad(shaped, ((0, 0), (margin, margin), (0, 0)))
    rows_out = []
    for step in range(width):
        rows_out.append(jnp.sum(grad_shaped * padded[:, step : step + frames], axis=(0, 1)))
    return jnp.stack(rows_out, 0)


def contract_rows(left, right):
    return lax.dot_general(
        left, right, (((0,), (0,)), ((), ())), preferred_element_type=jnp.float32
    )


MESH = pl.DeviceIdType.MESH
F32 = jnp.float32
BF16 = jnp.bfloat16
VMEM = pl.BlockSpec(memory_space=pltpu.VMEM)
DMA = pltpu.SemaphoreType.DMA
LIMIT = 56 * 1024 * 1024


def greet(axes):
    barrier = pltpu.get_barrier_semaphore()
    total = 0
    for axis in axes:
        size, me = lax.axis_size(axis), lax.axis_index(axis)
        for k in range(1, size):
            pl.semaphore_signal(
                barrier, inc=1, device_id={axis: lax.rem(me + k, size)}, device_id_type=MESH
            )
        total += size - 1
    pl.semaphore_wait(barrier, total)


def push(src, dst, send, recv, axis, peer):
    copy = pltpu.make_async_remote_copy(
        src_ref=src,
        dst_ref=dst,
        send_sem=send,
        recv_sem=recv,
        device_id={axis: peer},
        device_id_type=MESH,
    )
    copy.start()
    return copy


def push_all(axis, source, slots, send, recv):
    size, me = lax.axis_size(axis), lax.axis_index(axis)
    copies = []
    for k in range(1, size):
        peer = lax.rem(me + k, size)
        copies.append(push(source(peer), slots.at[me], send.at[k], recv.at[k], axis, peer))
    return copies


def sum_slots(slots, size):
    total = slots[0]
    for p in range(1, size):
        total = total + slots[p]
    return total


def stats_kernel(x_ref, o_ref, slots, send, recv):
    size, me = lax.axis_size("dp"), lax.axis_index("dp")
    greet(("dp",))
    copies = push_all("dp", lambda peer: x_ref, slots, send, recv)
    slots[me] = x_ref[...]
    for copy in copies:
        copy.wait()
    o_ref[...] = sum_slots(slots, size)


def stats_sum(row, cid):
    n = lax.axis_size("dp")
    return pl.pallas_call(
        stats_kernel,
        out_shape=jax.ShapeDtypeStruct(row.shape, F32),
        in_specs=[VMEM],
        out_specs=VMEM,
        scratch_shapes=[pltpu.VMEM((n,) + row.shape, F32), DMA((n,)), DMA((n,))],
        compiler_params=pltpu.CompilerParams(collective_id=cid, has_side_effects=True),
        name="stats_sum",
    )(row)


def grads_kernel(
    n,
    g1,
    g2,
    gk,
    o1,
    o2,
    ok,
    r1a,
    r1b,
    s1a,
    acc1,
    r2a,
    s2a,
    r3a,
    s1b,
    r2b,
    acc2,
    s2b,
    r3b,
    kslots,
    ksum,
    kall,
    core_sem,
    xa_sem,
    za_sem,
    zb_sem,
    xb_sem,
    k_sem,
    k2_sem,
):
    m = n // 4
    me = lax.axis_index("dp")
    c = lax.rem(me, 2)
    b = lax.rem(me // 2, 2)
    a = me // 4
    core_peer = me + 1 - 2 * c
    x_peer = me + 2 - 4 * b
    greet(("dp",))

    copy_1a = push(g1.at[:, :, 1 - c], r1a, core_sem.at[0, 0], core_sem.at[1, 0], "dp", core_peer)
    copy_1b = push(g2.at[:, :, 1 - c], r1b, core_sem.at[0, 1], core_sem.at[1, 1], "dp", core_peer)
    k_copies = push_all("dp", lambda peer: gk.at[peer], kslots, k_sem.at[0], k_sem.at[1])
    kslots[me] = gk[me]

    order = [lax.rem(a + k, m) for k in range(m)]
    steps = list(range(1, m)) + [0]

    copy_1a.wait_recv()
    xa = {}
    for k in steps:
        to = order[k]
        s1a[to] = (
            g1[to, 1 - b, c].astype(F32) + r1a[to, 1 - b].astype(F32)
        ).astype(BF16)
        xa[k] = push(s1a.at[to], r2a.at[to], xa_sem.at[0, k], xa_sem.at[1, k], "dp", x_peer)
    copy_1b.wait_recv()
    zb = []
    for k in steps:
        to = order[k]
        if k == 0:
            for j in range(2):
                acc2[j] = g2[to, j, c].astype(F32) + r1b[to, j].astype(F32)
            continue
        for j in range(2):
            s1b[to, j] = (g2[to, j, c].astype(F32) + r1b[to, j].astype(F32)).astype(BF16)
        peer = to * 4 + b * 2 + c
        zb.append(push(s1b.at[to], r2b.at[a], zb_sem.at[0, k], zb_sem.at[1, k], "dp", peer))
    for k in steps:
        to = order[k]
        acc1[to] = g1[to, b, c].astype(F32) + r1a[to, b].astype(F32)

    for copy in k_copies:
        copy.wait()
    ksum[...] = sum_slots(kslots, n)
    k2_copies = push_all("dp", lambda peer: ksum, kall, k2_sem.at[0], k2_sem.at[1])
    kall[me] = ksum[...]

    za = []
    for k in steps:
        to = order[k]
        xa[k].wait()
        if k == 0:
            continue
        s2a[to] = (acc1[to] + r2a[to].astype(F32)).astype(BF16)
        peer = to * 4 + b * 2 + c
        za.append(push(s2a.at[to], r3a.at[a], za_sem.at[0, k], za_sem.at[1, k], "dp", peer))

    for copy in zb:
        copy.wait()
    for k in range(1, m):
        frm = lax.rem(a - k + m, m)
        for j in range(2):
            acc2[j] = acc2[j] + r2b[frm, j].astype(F32)
    s2b[...] = acc2[1 - b].astype(BF16)
    xb = push(s2b, r3b, xb_sem.at[0], xb_sem.at[1], "dp", x_peer)

    o1[...] = acc1[a] + r2a[a].astype(F32)
    for copy in k2_copies:
        copy.wait()
    ok[...] = kall[...]
    xb.wait()
    o2[...] = acc2[b] + r3b[...].astype(F32)
    for copy in za:
        copy.wait()
    total = o1[...]
    for k in range(1, m):
        total = total + r3a[lax.rem(a - k + m, m)].astype(F32)
    o1[...] = total
    copy_1a.wait_send()
    copy_1b.wait_send()


def grads_sum(g1, g2, gk, cid):
    n = lax.axis_size("dp")
    m = n // 4
    rows, wide = g1.shape[0] // n, g1.shape[1]
    chans = g2.shape[1]
    flat = gk.reshape(-1)
    part = -(-flat.shape[0] // (n * 128)) * 128
    flat = jnp.pad(flat, (0, n * part - flat.shape[0])).reshape(n, 1, part)
    o1, o2, ok = pl.pallas_call(
        functools.partial(grads_kernel, n),
        out_shape=(
            jax.ShapeDtypeStruct((rows, wide), F32),
            jax.ShapeDtypeStruct((rows, chans), F32),
            jax.ShapeDtypeStruct((n, 1, part), F32),
        ),
        in_specs=[VMEM] * 3,
        out_specs=(VMEM,) * 3,
        scratch_shapes=[
            pltpu.VMEM((m, 2, rows, wide), BF16),
            pltpu.VMEM((m, 2, rows, chans), BF16),
            pltpu.VMEM((m, rows, wide), BF16),
            pltpu.VMEM((m, rows, wide), F32),
            pltpu.VMEM((m, rows, wide), BF16),
            pltpu.VMEM((m, rows, wide), BF16),
            pltpu.VMEM((m, rows, wide), BF16),
            pltpu.VMEM((m, 2, rows, chans), BF16),
            pltpu.VMEM((m, 2, rows, chans), BF16),
            pltpu.VMEM((2, rows, chans), F32),
            pltpu.VMEM((rows, chans), BF16),
            pltpu.VMEM((rows, chans), BF16),
            pltpu.VMEM((n, 1, part), F32),
            pltpu.VMEM((1, part), F32),
            pltpu.VMEM((n, 1, part), F32),
            DMA((2, 2)),
            DMA((2, m)),
            DMA((2, m)),
            DMA((2, m)),
            DMA((2,)),
            DMA((2, n)),
            DMA((2, n)),
        ],
        compiler_params=pltpu.CompilerParams(
            collective_id=cid, has_side_effects=True, vmem_limit_bytes=LIMIT
        ),
        name="grads_sum",
    )(
        g1.reshape(m, 2, 2, rows, wide),
        g2.reshape(m, 2, 2, rows, chans),
        flat,
    )
    return o1, o2, ok.reshape(-1)[: gk.size].reshape(gk.shape)


def spread_kernel(
    n, w1, w2, pk, rt, gn, f1, f2, rec, rts, gns, z_sem, x_sem, core_sem, p_sem, r_sem, g_sem
):
    m = n // 4
    me, mine = lax.axis_index("dp"), lax.axis_index("mp")
    c = lax.rem(me, 2)
    b = lax.rem(me // 2, 2)
    a = me // 4
    core_peer = me + 1 - 2 * c
    x_peer = me + 2 - 4 * b
    greet(("dp", "mp"))
    small = push_all("dp", lambda peer: pk.at[peer], rec, p_sem.at[0], p_sem.at[1])
    small += push_all("mp", lambda peer: rt, rts, r_sem.at[0], r_sem.at[1])
    small += push_all("mp", lambda peer: gn, gns, g_sem.at[0], g_sem.at[1])
    owns, full = (w1, w2), (f1, f2)

    def spot(line, row):
        return line * 4 + row * 2 + c

    def copy_of(src, i, at, sems, index, peer):
        return pltpu.make_async_remote_copy(
            src_ref=src,
            dst_ref=full[i].at[at],
            send_sem=sems.at[i, 0, index],
            recv_sem=sems.at[i, 1, index],
            device_id={"dp": peer},
            device_id_type=MESH,
        )

    def has(way, k):
        return a >= k if way == 0 else a + k < m

    def source(way, k):
        return a - k if way == 0 else a + k

    def passes(way):
        return a + 1 < m if way == 0 else a >= 1

    def z_copy(i, src, at, way, hop):
        peer = spot(a + 1, b) if way == 0 else spot(a - 1, b)
        return copy_of(src, i, at, z_sem, way * m + hop, peer)

    def x_copy(i, src, at, index):
        return copy_of(src, i, at, x_sem, index, x_peer)

    def core_copy(i, src, at, index):
        return copy_of(src, i, at, core_sem, index, core_peer)

    def begin(i):
        for way in range(2):

            @pl.when(passes(way))
            def _():
                z_copy(i, owns[i], me, way, 1).start()

        x_copy(i, owns[i], me, 0).start()
        core_copy(i, owns[i], me, 0).start()

    def z_step(i, k, way):
        @pl.when(has(way, k))
        def _():
            at = spot(source(way, k), b)
            block = full[i].at[at]
            z_copy(i, owns[i], me, way, k).wait_recv()
            if k < m - 1:

                @pl.when(passes(way))
                def _():
                    z_copy(i, block, at, way, k + 1).start()

            x_copy(i, block, at, way * m + k).start()
            core_copy(i, block, at, way * m + k).start()

    def x_step(i, k, way):
        @pl.when(has(way, k))
        def _():
            at = spot(source(way, k), 1 - b)
            x_copy(i, owns[i], me, way * m + k).wait_recv()
            core_copy(i, full[i].at[at], at, (2 + way) * m + k).start()

    def finish(i):
        for way in range(2):

            @pl.when(passes(way))
            def _():
                z_copy(i, owns[i], me, way, 1).wait_send()

        for k in range(m):
            for way in range(2 if k else 1):

                @pl.when(has(way, k))
                def _():
                    if 0 < k < m - 1:

                        @pl.when(passes(way))
                        def _():
                            z_copy(i, owns[i], me, way, k + 1).wait_send()

                    x_copy(i, owns[i], me, way * m + k).wait_send()
                    core_copy(i, owns[i], me, way * m + k).wait()
                    core_copy(i, owns[i], me, (2 + way) * m + k).wait()

    begin(0)
    f1[me] = w1[...]
    f2[me] = w2[...]
    rec[me] = pk[me]
    rts[mine] = rt[...]
    gns[mine] = gn[...]
    for k in range(1, m):
        for way in range(2):
            z_step(0, k, way)
        if k == 1:
            begin(1)
            x_step(0, 0, 0)
        else:
            for way in range(2):
                x_step(0, k - 1, way)
    for k in range(1, m):
        for way in range(2):
            z_step(1, k, way)
        if k == 1:
            for way in range(2):
                x_step(0, m - 1, way)
    x_step(1, 0, 0)
    for k in range(1, m):
        for way in range(2):
            x_step(1, k, way)
    for copy in small:
        copy.wait()
    for i in range(2):
        finish(i)


def spread(w1, w2, packed, right, gain, cid):
    n, q = lax.axis_size("dp"), lax.axis_size("mp")
    m = n // 4
    return pl.pallas_call(
        functools.partial(spread_kernel, n),
        out_shape=(
            jax.ShapeDtypeStruct((n,) + w1.shape, BF16),
            jax.ShapeDtypeStruct((n,) + w2.shape, BF16),
            jax.ShapeDtypeStruct(packed.shape, BF16),
            jax.ShapeDtypeStruct((q,) + right.shape, BF16),
            jax.ShapeDtypeStruct((q,) + gain.shape, F32),
        ),
        in_specs=[VMEM] * 5,
        out_specs=(VMEM,) * 5,
        scratch_shapes=[
            DMA((2, 2, 2 * m)),
            DMA((2, 2, 2 * m)),
            DMA((2, 2, 4 * m)),
            DMA((2, n)),
            DMA((2, q)),
            DMA((2, q)),
        ],
        compiler_params=pltpu.CompilerParams(
            collective_id=cid, has_side_effects=True, vmem_limit_bytes=LIMIT
        ),
        name="spread",
    )(w1, w2, packed, right, gain)


def on_device(
    corpus,
    picks,
    lengths,
    langs,
    w_in,
    lang_table,
    ln_gain,
    w_pw1,
    kernel,
    bn_gain,
    bn_bias,
    w_pw2,
    cotangent,
):
    model_width = w_pw2.shape[0] * lax.axis_size("dp")
    parts = lax.axis_size("mp")
    half = w_pw2.shape[1]
    feats = corpus.shape[2]
    frames = corpus.shape[1]
    picked = picks[0][:, None] == jnp.arange(corpus.shape[0], dtype=jnp.int32)[None, :]
    blocks = jnp.einsum(
        "sb,bfk->sfk", picked.astype(BF16), corpus, preferred_element_type=F32
    ).astype(BF16)
    lens_send = jnp.sum(jnp.where(picked, lengths[None, :], 0), 1)
    lang_send = jnp.sum(jnp.where(picked, langs[None, :], 0), 1)
    whole = jnp.stack([lens_send, lang_send], 1).astype(BF16)
    whole = jnp.broadcast_to(whole[:, None, :], (whole.shape[0], frames, 2))
    lanes = -(-(feats + 2) // 128) * 128
    spare = jnp.zeros((whole.shape[0], frames, lanes - feats - 2), BF16)
    packed = jnp.concatenate([blocks, whole, spare], 2)
    right = jnp.concatenate([w_in, lang_table], 0)
    weights_one, weights_two, received, right_full, gain_full = spread(
        w_pw1.reshape(w_pw1.shape[0], -1), w_pw2, packed, right, ln_gain[None], 4
    )
    weights_one = weights_one.reshape(model_width, -1)
    weights_two = weights_two.reshape(model_width, -1)
    lens = received[:, 0, feats].astype(jnp.int32)
    lang = received[:, 0, feats + 1].astype(jnp.int32)
    valid = (
        (jnp.arange(frames, dtype=jnp.int32)[None, :] < lens[:, None]).astype(F32).reshape(-1)
    )
    valid_col = valid[:, None]
    mel = received[:, :, :feats].reshape(-1, feats) * valid_col.astype(BF16)
    onehot = (lang[:, None] == jnp.arange(lang_table.shape[0], dtype=jnp.int32)[None, :]).astype(
        BF16
    )
    onehot = jnp.repeat(onehot, frames, axis=0)
    left = jnp.concatenate([mel, onehot], 1)
    inputs = jnp.dot(left, right, preferred_element_type=F32)
    full_in = jnp.concatenate(
        [jnp.dot(left, right_full[p], preferred_element_type=F32) for p in range(parts)], 1
    )
    gain_full = gain_full.reshape(-1)
    mean = jnp.sum(full_in, 1) / model_width
    var = jnp.sum(full_in * full_in, 1) / model_width - mean * mean
    normed_full = (
        (full_in - mean[:, None]) * lax.rsqrt(var + EPS)[:, None] * gain_full
    ).astype(BF16)
    pre = jnp.dot(normed_full, weights_one, preferred_element_type=jnp.float32)
    linear_part = pre[:, :half]
    gate_part = pre[:, half:]
    gate_sig = jax.nn.sigmoid(gate_part)
    glu_out = linear_part * gate_sig * valid_col
    conv_out = depth_conv(glu_out, kernel, frames)
    row = jnp.concatenate(
        [
            jnp.sum(valid_col * conv_out, 0),
            jnp.sum(valid_col * conv_out * conv_out, 0),
            jnp.full((128,), jnp.sum(valid), F32),
        ]
    )[None]
    row = stats_sum(row, 1)
    sum_conv, sum_sq, count = row[0, :half], row[0, half : 2 * half], row[0, 2 * half]
    mu_conv = sum_conv / count
    var_conv = sum_sq / count - mu_conv * mu_conv
    inv_std = lax.rsqrt(var_conv + EPS)
    normed_conv = (conv_out - mu_conv) * inv_std
    act = normed_conv * bn_gain + bn_bias
    act_sig = jax.nn.sigmoid(act)
    hidden = (valid_col * act * act_sig).astype(jnp.bfloat16)
    partial = lax.dot_general(
        cotangent, weights_two, (((1,), (1,)), ((), ())), preferred_element_type=F32
    ).astype(BF16)
    partial = jnp.stack([partial[:, p * half : (p + 1) * half] for p in range(parts)], 0)
    partial = lax.all_to_all(partial, "mp", split_axis=0, concat_axis=0, tiled=True)
    dhidden = jnp.sum(partial.astype(F32), 0)
    dact = dhidden * valid_col * act_sig * (1.0 + act * (1.0 - act_sig))
    row2 = jnp.concatenate([jnp.sum(dact, 0), jnp.sum(dact * normed_conv, 0)])[None]
    row2 = stats_sum(row2, 2)
    mine = lax.axis_index("mp")
    held = [hidden] + [
        lax.ppermute(hidden, "mp", [(i, (i + k) % parts) for i in range(parts)])
        for k in range(1, parts)
    ]
    placed = []
    for p in range(parts):
        block = held[0]
        for k in range(1, parts):
            block = jnp.where(lax.rem(mine - p + parts, parts) == k, held[k], block)
        placed.append(block)
    hidden_full = jnp.concatenate(placed, 1)
    grad_bias, grad_gain = row2[0, :half], row2[0, half:]
    encoded = (inputs + jnp.dot(hidden_full, weights_two, preferred_element_type=F32)).astype(
        BF16
    )
    part_pw2 = contract_rows(hidden_full, cotangent).astype(BF16)
    dconv = (
        valid_col * inv_std * bn_gain * (dact - grad_bias / count - normed_conv * grad_gain / count)
    )
    part_kernel = kernel_terms(dconv, glu_out, kernel.shape[0], frames)
    dglu = depth_back(dconv, kernel, frames)
    dlin = dglu * valid_col * gate_sig
    dgate = dglu * valid_col * linear_part * gate_sig * (1.0 - gate_sig)
    dpre = jnp.concatenate([dlin, dgate], 1).astype(jnp.bfloat16)
    part_pw1 = contract_rows(normed_full, dpre).astype(BF16)
    grad_pw1, grad_pw2, grad_kernel = grads_sum(part_pw1, part_pw2, part_kernel, 3)
    grad_pw1 = grad_pw1.reshape(grad_pw1.shape[0], 2, half)
    return (encoded, grad_pw1, grad_pw2, grad_kernel, grad_gain, grad_bias)


def solution(mesh):
    return jax.shard_map(
        on_device,
        mesh=mesh,
        in_specs=(
            P("dp", None, None),
            P("dp", None),
            P("dp"),
            P("dp"),
            P(None, "mp"),
            P(None, "mp"),
            P("mp"),
            P("dp", None, "mp"),
            P(None, "mp"),
            P("mp"),
            P("mp"),
            P("dp", "mp"),
            P("dp", "mp"),
        ),
        out_specs=(
            P("dp", "mp"),
            P("dp", None, "mp"),
            P("dp", "mp"),
            P(None, "mp"),
            P("mp"),
            P("mp"),
        ),
        check_vma=False,
    )
```

```python
import functools

import jax
import jax.numpy as jnp
from jax import lax
from jax.experimental import pallas as pl
from jax.experimental.pallas import tpu as pltpu
from jax.sharding import PartitionSpec as P

EPS = 1e-05


def depth_conv(values, taps, frames):
    chans = values.shape[1]
    shaped = values.reshape(-1, frames, chans)
    margin = taps.shape[0] // 2
    padded = jnp.pad(shaped, ((0, 0), (margin, margin), (0, 0)))
    total = jnp.zeros(shaped.shape, jnp.float32)
    for step in range(taps.shape[0]):
        total = total + taps[step] * padded[:, step : step + frames]
    return total.reshape(values.shape)


def depth_back(grads, taps, frames):
    chans = grads.shape[1]
    shaped = grads.reshape(-1, frames, chans)
    margin = taps.shape[0] // 2
    padded = jnp.pad(shaped, ((0, 0), (margin, margin), (0, 0)))
    total = jnp.zeros(shaped.shape, jnp.float32)
    for step in range(taps.shape[0]):
        begin = 2 * margin - step
        total = total + taps[step] * padded[:, begin : begin + frames]
    return total.reshape(grads.shape)


def kernel_terms(grads, values, width, frames):
    chans = values.shape[1]
    shaped = values.reshape(-1, frames, chans)
    grad_shaped = grads.reshape(-1, frames, chans)
    margin = width // 2
    padded = jnp.pad(shaped, ((0, 0), (margin, margin), (0, 0)))
    rows_out = []
    for step in range(width):
        rows_out.append(jnp.sum(grad_shaped * padded[:, step : step + frames], axis=(0, 1)))
    return jnp.stack(rows_out, 0)


def contract_rows(left, right):
    return lax.dot_general(
        left, right, (((0,), (0,)), ((), ())), preferred_element_type=jnp.float32
    )


MESH = pl.DeviceIdType.MESH
F32 = jnp.float32
BF16 = jnp.bfloat16
VMEM = pl.BlockSpec(memory_space=pltpu.VMEM)
DMA = pltpu.SemaphoreType.DMA
LIMIT = 56 * 1024 * 1024


def greet(axes):
    barrier = pltpu.get_barrier_semaphore()
    total = 0
    for axis in axes:
        size, me = lax.axis_size(axis), lax.axis_index(axis)
        for k in range(1, size):
            pl.semaphore_signal(
                barrier, inc=1, device_id={axis: lax.rem(me + k, size)}, device_id_type=MESH
            )
        total += size - 1
    pl.semaphore_wait(barrier, total)


def push(src, dst, send, recv, axis, peer):
    copy = pltpu.make_async_remote_copy(
        src_ref=src,
        dst_ref=dst,
        send_sem=send,
        recv_sem=recv,
        device_id={axis: peer},
        device_id_type=MESH,
    )
    copy.start()
    return copy


def push_all(axis, source, slots, send, recv):
    size, me = lax.axis_size(axis), lax.axis_index(axis)
    copies = []
    for k in range(1, size):
        peer = lax.rem(me + k, size)
        copies.append(push(source(peer), slots.at[me], send.at[k], recv.at[k], axis, peer))
    return copies


def sum_slots(slots, size):
    total = slots[0]
    for p in range(1, size):
        total = total + slots[p]
    return total


def stats_kernel(x_ref, o_ref, slots, send, recv):
    size, me = lax.axis_size("dp"), lax.axis_index("dp")
    greet(("dp",))
    copies = push_all("dp", lambda peer: x_ref, slots, send, recv)
    slots[me] = x_ref[...]
    for copy in copies:
        copy.wait()
    o_ref[...] = sum_slots(slots, size)


def stats_sum(row, cid):
    n = lax.axis_size("dp")
    return pl.pallas_call(
        stats_kernel,
        out_shape=jax.ShapeDtypeStruct(row.shape, F32),
        in_specs=[VMEM],
        out_specs=VMEM,
        scratch_shapes=[pltpu.VMEM((n,) + row.shape, F32), DMA((n,)), DMA((n,))],
        compiler_params=pltpu.CompilerParams(collective_id=cid, has_side_effects=True),
        name="stats_sum",
    )(row)


def stats_hidden_kernel(
    x_ref, h_ref, o_ref, hid_ref, slots, hslots, send, recv, hsend, hrecv
):
    size, me = lax.axis_size("dp"), lax.axis_index("dp")
    parts, mine = lax.axis_size("mp"), lax.axis_index("mp")
    chans = h_ref.shape[1]
    greet(("dp", "mp"))
    copies = push_all("dp", lambda peer: x_ref, slots, send, recv)
    wide = push_all("mp", lambda peer: h_ref, hslots, hsend, hrecv)
    slots[me] = x_ref[...]
    hslots[mine] = h_ref[...]
    for copy in copies:
        copy.wait()
    o_ref[...] = sum_slots(slots, size)
    for copy in wide:
        copy.wait()
    for p in range(parts):
        hid_ref[:, p * chans : (p + 1) * chans] = hslots[p]


def stats_hidden(row, hidden, cid):
    n, q = lax.axis_size("dp"), lax.axis_size("mp")
    rows, chans = hidden.shape
    return pl.pallas_call(
        stats_hidden_kernel,
        out_shape=(
            jax.ShapeDtypeStruct(row.shape, F32),
            jax.ShapeDtypeStruct((rows, q * chans), BF16),
        ),
        in_specs=[VMEM, VMEM],
        out_specs=(VMEM, VMEM),
        scratch_shapes=[
            pltpu.VMEM((n,) + row.shape, F32),
            pltpu.VMEM((q,) + hidden.shape, BF16),
            DMA((n,)),
            DMA((n,)),
            DMA((q,)),
            DMA((q,)),
        ],
        compiler_params=pltpu.CompilerParams(
            collective_id=cid, has_side_effects=True, vmem_limit_bytes=LIMIT
        ),
        name="stats_hidden",
    )(row, hidden)


def grads_kernel(
    n,
    g1,
    g2,
    gk,
    o1,
    o2,
    ok,
    r1a,
    r1b,
    s1a,
    acc1,
    r2a,
    s2a,
    r3a,
    s1b,
    r2b,
    acc2,
    s2b,
    r3b,
    kslots,
    ksum,
    kall,
    core_sem,
    xa_sem,
    za_sem,
    zb_sem,
    xb_sem,
    k_sem,
    k2_sem,
):
    m = n // 4
    me = lax.axis_index("dp")
    c = lax.rem(me, 2)
    b = lax.rem(me // 2, 2)
    a = me // 4
    core_peer = me + 1 - 2 * c
    x_peer = me + 2 - 4 * b
    greet(("dp",))

    copy_1a = push(g1.at[:, :, 1 - c], r1a, core_sem.at[0, 0], core_sem.at[1, 0], "dp", core_peer)
    copy_1b = push(g2.at[:, :, 1 - c], r1b, core_sem.at[0, 1], core_sem.at[1, 1], "dp", core_peer)
    k_copies = push_all("dp", lambda peer: gk.at[peer], kslots, k_sem.at[0], k_sem.at[1])
    kslots[me] = gk[me]

    order = [lax.rem(a + k, m) for k in range(m)]
    steps = list(range(1, m)) + [0]

    copy_1a.wait_recv()
    xa = {}
    for k in steps:
        to = order[k]
        s1a[to] = (
            g1[to, 1 - b, c].astype(F32) + r1a[to, 1 - b].astype(F32)
        ).astype(BF16)
        xa[k] = push(s1a.at[to], r2a.at[to], xa_sem.at[0, k], xa_sem.at[1, k], "dp", x_peer)
    copy_1b.wait_recv()
    zb = []
    for k in steps:
        to = order[k]
        if k == 0:
            for j in range(2):
                acc2[j] = g2[to, j, c].astype(F32) + r1b[to, j].astype(F32)
            continue
        for j in range(2):
            s1b[to, j] = (g2[to, j, c].astype(F32) + r1b[to, j].astype(F32)).astype(BF16)
        peer = to * 4 + b * 2 + c
        zb.append(push(s1b.at[to], r2b.at[a], zb_sem.at[0, k], zb_sem.at[1, k], "dp", peer))
    for k in steps:
        to = order[k]
        acc1[to] = g1[to, b, c].astype(F32) + r1a[to, b].astype(F32)

    for copy in k_copies:
        copy.wait()
    ksum[...] = sum_slots(kslots, n)
    k2_copies = push_all("dp", lambda peer: ksum, kall, k2_sem.at[0], k2_sem.at[1])
    kall[me] = ksum[...]

    za = []
    for k in steps:
        to = order[k]
        xa[k].wait()
        if k == 0:
            continue
        s2a[to] = (acc1[to] + r2a[to].astype(F32)).astype(BF16)
        peer = to * 4 + b * 2 + c
        za.append(push(s2a.at[to], r3a.at[a], za_sem.at[0, k], za_sem.at[1, k], "dp", peer))

    for copy in zb:
        copy.wait()
    for k in range(1, m):
        frm = lax.rem(a - k + m, m)
        for j in range(2):
            acc2[j] = acc2[j] + r2b[frm, j].astype(F32)
    s2b[...] = acc2[1 - b].astype(BF16)
    xb = push(s2b, r3b, xb_sem.at[0], xb_sem.at[1], "dp", x_peer)

    o1[...] = acc1[a] + r2a[a].astype(F32)
    for copy in k2_copies:
        copy.wait()
    ok[...] = kall[...]
    xb.wait()
    o2[...] = acc2[b] + r3b[...].astype(F32)
    for copy in za:
        copy.wait()
    total = o1[...]
    for k in range(1, m):
        total = total + r3a[lax.rem(a - k + m, m)].astype(F32)
    o1[...] = total
    copy_1a.wait_send()
    copy_1b.wait_send()


def grads_sum(g1, g2, gk, cid):
    n = lax.axis_size("dp")
    m = n // 4
    rows, wide = g1.shape[0] // n, g1.shape[1]
    chans = g2.shape[1]
    flat = gk.reshape(-1)
    part = -(-flat.shape[0] // (n * 128)) * 128
    flat = jnp.pad(flat, (0, n * part - flat.shape[0])).reshape(n, 1, part)
    o1, o2, ok = pl.pallas_call(
        functools.partial(grads_kernel, n),
        out_shape=(
            jax.ShapeDtypeStruct((rows, wide), F32),
            jax.ShapeDtypeStruct((rows, chans), F32),
            jax.ShapeDtypeStruct((n, 1, part), F32),
        ),
        in_specs=[VMEM] * 3,
        out_specs=(VMEM,) * 3,
        scratch_shapes=[
            pltpu.VMEM((m, 2, rows, wide), BF16),
            pltpu.VMEM((m, 2, rows, chans), BF16),
            pltpu.VMEM((m, rows, wide), BF16),
            pltpu.VMEM((m, rows, wide), F32),
            pltpu.VMEM((m, rows, wide), BF16),
            pltpu.VMEM((m, rows, wide), BF16),
            pltpu.VMEM((m, rows, wide), BF16),
            pltpu.VMEM((m, 2, rows, chans), BF16),
            pltpu.VMEM((m, 2, rows, chans), BF16),
            pltpu.VMEM((2, rows, chans), F32),
            pltpu.VMEM((rows, chans), BF16),
            pltpu.VMEM((rows, chans), BF16),
            pltpu.VMEM((n, 1, part), F32),
            pltpu.VMEM((1, part), F32),
            pltpu.VMEM((n, 1, part), F32),
            DMA((2, 2)),
            DMA((2, m)),
            DMA((2, m)),
            DMA((2, m)),
            DMA((2,)),
            DMA((2, n)),
            DMA((2, n)),
        ],
        compiler_params=pltpu.CompilerParams(
            collective_id=cid, has_side_effects=True, vmem_limit_bytes=LIMIT
        ),
        name="grads_sum",
    )(
        g1.reshape(m, 2, 2, rows, wide),
        g2.reshape(m, 2, 2, rows, chans),
        flat,
    )
    return o1, o2, ok.reshape(-1)[: gk.size].reshape(gk.shape)


def spread_kernel(
    n, w1, w2, pk, rt, gn, f1, f2, rec, rts, gns, z_sem, x_sem, core_sem, p_sem, r_sem, g_sem
):
    m = n // 4
    me, mine = lax.axis_index("dp"), lax.axis_index("mp")
    c = lax.rem(me, 2)
    b = lax.rem(me // 2, 2)
    a = me // 4
    core_peer = me + 1 - 2 * c
    x_peer = me + 2 - 4 * b
    greet(("dp", "mp"))
    small = push_all("dp", lambda peer: pk.at[peer], rec, p_sem.at[0], p_sem.at[1])
    small += push_all("mp", lambda peer: rt, rts, r_sem.at[0], r_sem.at[1])
    small += push_all("mp", lambda peer: gn, gns, g_sem.at[0], g_sem.at[1])
    owns, full = (w1, w2), (f1, f2)

    def spot(line, row):
        return line * 4 + row * 2 + c

    def copy_of(src, i, at, sems, index, peer):
        return pltpu.make_async_remote_copy(
            src_ref=src,
            dst_ref=full[i].at[at],
            send_sem=sems.at[i, 0, index],
            recv_sem=sems.at[i, 1, index],
            device_id={"dp": peer},
            device_id_type=MESH,
        )

    def has(way, k):
        return a >= k if way == 0 else a + k < m

    def source(way, k):
        return a - k if way == 0 else a + k

    def passes(way):
        return a + 1 < m if way == 0 else a >= 1

    def z_copy(i, src, at, way, hop):
        peer = spot(a + 1, b) if way == 0 else spot(a - 1, b)
        return copy_of(src, i, at, z_sem, way * m + hop, peer)

    def x_copy(i, src, at, index):
        return copy_of(src, i, at, x_sem, index, x_peer)

    def core_copy(i, src, at, index):
        return copy_of(src, i, at, core_sem, index, core_peer)

    def begin(i):
        for way in range(2):

            @pl.when(passes(way))
            def _():
                z_copy(i, owns[i], me, way, 1).start()

        x_copy(i, owns[i], me, 0).start()
        core_copy(i, owns[i], me, 0).start()

    def z_step(i, k, way):
        @pl.when(has(way, k))
        def _():
            at = spot(source(way, k), b)
            block = full[i].at[at]
            z_copy(i, owns[i], me, way, k).wait_recv()
            if k < m - 1:

                @pl.when(passes(way))
                def _():
                    z_copy(i, block, at, way, k + 1).start()

            x_copy(i, block, at, way * m + k).start()
            core_copy(i, block, at, way * m + k).start()

    def x_step(i, k, way):
        @pl.when(has(way, k))
        def _():
            at = spot(source(way, k), 1 - b)
            x_copy(i, owns[i], me, way * m + k).wait_recv()
            core_copy(i, full[i].at[at], at, (2 + way) * m + k).start()

    def finish(i):
        for way in range(2):

            @pl.when(passes(way))
            def _():
                z_copy(i, owns[i], me, way, 1).wait_send()

        for k in range(m):
            for way in range(2 if k else 1):

                @pl.when(has(way, k))
                def _():
                    if 0 < k < m - 1:

                        @pl.when(passes(way))
                        def _():
                            z_copy(i, owns[i], me, way, k + 1).wait_send()

                    x_copy(i, owns[i], me, way * m + k).wait_send()
                    core_copy(i, owns[i], me, way * m + k).wait()
                    core_copy(i, owns[i], me, (2 + way) * m + k).wait()

    begin(0)
    f1[me] = w1[...]
    f2[me] = w2[...]
    rec[me] = pk[me]
    rts[mine] = rt[...]
    gns[mine] = gn[...]
    for k in range(1, m):
        for way in range(2):
            z_step(0, k, way)
        if k == 1:
            begin(1)
            x_step(0, 0, 0)
        else:
            for way in range(2):
                x_step(0, k - 1, way)
    for k in range(1, m):
        for way in range(2):
            z_step(1, k, way)
        if k == 1:
            for way in range(2):
                x_step(0, m - 1, way)
    x_step(1, 0, 0)
    for k in range(1, m):
        for way in range(2):
            x_step(1, k, way)
    for copy in small:
        copy.wait()
    for i in range(2):
        finish(i)


def spread(w1, w2, packed, right, gain, cid):
    n, q = lax.axis_size("dp"), lax.axis_size("mp")
    m = n // 4
    return pl.pallas_call(
        functools.partial(spread_kernel, n),
        out_shape=(
            jax.ShapeDtypeStruct((n,) + w1.shape, BF16),
            jax.ShapeDtypeStruct((n,) + w2.shape, BF16),
            jax.ShapeDtypeStruct(packed.shape, BF16),
            jax.ShapeDtypeStruct((q,) + right.shape, BF16),
            jax.ShapeDtypeStruct((q,) + gain.shape, F32),
        ),
        in_specs=[VMEM] * 5,
        out_specs=(VMEM,) * 5,
        scratch_shapes=[
            DMA((2, 2, 2 * m)),
            DMA((2, 2, 2 * m)),
            DMA((2, 2, 4 * m)),
            DMA((2, n)),
            DMA((2, q)),
            DMA((2, q)),
        ],
        compiler_params=pltpu.CompilerParams(
            collective_id=cid, has_side_effects=True, vmem_limit_bytes=LIMIT
        ),
        name="spread",
    )(w1, w2, packed, right, gain)


def on_device(
    corpus,
    picks,
    lengths,
    langs,
    w_in,
    lang_table,
    ln_gain,
    w_pw1,
    kernel,
    bn_gain,
    bn_bias,
    w_pw2,
    cotangent,
):
    model_width = w_pw2.shape[0] * lax.axis_size("dp")
    parts = lax.axis_size("mp")
    half = w_pw2.shape[1]
    feats = corpus.shape[2]
    frames = corpus.shape[1]
    picked = picks[0][:, None] == jnp.arange(corpus.shape[0], dtype=jnp.int32)[None, :]
    blocks = jnp.einsum(
        "sb,bfk->sfk", picked.astype(BF16), corpus, preferred_element_type=F32
    ).astype(BF16)
    lens_send = jnp.sum(jnp.where(picked, lengths[None, :], 0), 1)
    lang_send = jnp.sum(jnp.where(picked, langs[None, :], 0), 1)
    whole = jnp.stack([lens_send, lang_send], 1).astype(BF16)
    whole = jnp.broadcast_to(whole[:, None, :], (whole.shape[0], frames, 2))
    lanes = -(-(feats + 2) // 128) * 128
    spare = jnp.zeros((whole.shape[0], frames, lanes - feats - 2), BF16)
    packed = jnp.concatenate([blocks, whole, spare], 2)
    right = jnp.concatenate([w_in, lang_table], 0)
    weights_one, weights_two, received, right_full, gain_full = spread(
        w_pw1.reshape(w_pw1.shape[0], -1), w_pw2, packed, right, ln_gain[None], 4
    )
    weights_one = weights_one.reshape(model_width, -1)
    weights_two = weights_two.reshape(model_width, -1)
    lens = received[:, 0, feats].astype(jnp.int32)
    lang = received[:, 0, feats + 1].astype(jnp.int32)
    valid = (
        (jnp.arange(frames, dtype=jnp.int32)[None, :] < lens[:, None]).astype(F32).reshape(-1)
    )
    valid_col = valid[:, None]
    mel = received[:, :, :feats].reshape(-1, feats) * valid_col.astype(BF16)
    onehot = (lang[:, None] == jnp.arange(lang_table.shape[0], dtype=jnp.int32)[None, :]).astype(
        BF16
    )
    onehot = jnp.repeat(onehot, frames, axis=0)
    left = jnp.concatenate([mel, onehot], 1)
    inputs = jnp.dot(left, right, preferred_element_type=F32)
    full_in = jnp.concatenate(
        [jnp.dot(left, right_full[p], preferred_element_type=F32) for p in range(parts)], 1
    )
    gain_full = gain_full.reshape(-1)
    mean = jnp.sum(full_in, 1) / model_width
    var = jnp.sum(full_in * full_in, 1) / model_width - mean * mean
    normed_full = (
        (full_in - mean[:, None]) * lax.rsqrt(var + EPS)[:, None] * gain_full
    ).astype(BF16)
    pre = jnp.dot(normed_full, weights_one, preferred_element_type=jnp.float32)
    linear_part = pre[:, :half]
    gate_part = pre[:, half:]
    gate_sig = jax.nn.sigmoid(gate_part)
    glu_out = linear_part * gate_sig * valid_col
    conv_out = depth_conv(glu_out, kernel, frames)
    row = jnp.concatenate(
        [
            jnp.sum(valid_col * conv_out, 0),
            jnp.sum(valid_col * conv_out * conv_out, 0),
            jnp.full((128,), jnp.sum(valid), F32),
        ]
    )[None]
    row = stats_sum(row, 1)
    sum_conv, sum_sq, count = row[0, :half], row[0, half : 2 * half], row[0, 2 * half]
    mu_conv = sum_conv / count
    var_conv = sum_sq / count - mu_conv * mu_conv
    inv_std = lax.rsqrt(var_conv + EPS)
    normed_conv = (conv_out - mu_conv) * inv_std
    act = normed_conv * bn_gain + bn_bias
    act_sig = jax.nn.sigmoid(act)
    hidden = (valid_col * act * act_sig).astype(jnp.bfloat16)
    partial = lax.dot_general(
        cotangent, weights_two, (((1,), (1,)), ((), ())), preferred_element_type=F32
    ).astype(BF16)
    partial = jnp.stack([partial[:, p * half : (p + 1) * half] for p in range(parts)], 0)
    partial = lax.all_to_all(partial, "mp", split_axis=0, concat_axis=0, tiled=True)
    dhidden = jnp.sum(partial.astype(F32), 0)
    dact = dhidden * valid_col * act_sig * (1.0 + act * (1.0 - act_sig))
    row2 = jnp.concatenate([jnp.sum(dact, 0), jnp.sum(dact * normed_conv, 0)])[None]
    row2, hidden_full = stats_hidden(row2, hidden, 2)
    grad_bias, grad_gain = row2[0, :half], row2[0, half:]
    encoded = (inputs + jnp.dot(hidden_full, weights_two, preferred_element_type=F32)).astype(
        BF16
    )
    part_pw2 = contract_rows(hidden_full, cotangent).astype(BF16)
    dconv = (
        valid_col * inv_std * bn_gain * (dact - grad_bias / count - normed_conv * grad_gain / count)
    )
    part_kernel = kernel_terms(dconv, glu_out, kernel.shape[0], frames)
    dglu = depth_back(dconv, kernel, frames)
    dlin = dglu * valid_col * gate_sig
    dgate = dglu * valid_col * linear_part * gate_sig * (1.0 - gate_sig)
    dpre = jnp.concatenate([dlin, dgate], 1).astype(jnp.bfloat16)
    part_pw1 = contract_rows(normed_full, dpre).astype(BF16)
    grad_pw1, grad_pw2, grad_kernel = grads_sum(part_pw1, part_pw2, part_kernel, 3)
    grad_pw1 = grad_pw1.reshape(grad_pw1.shape[0], 2, half)
    return (encoded, grad_pw1, grad_pw2, grad_kernel, grad_gain, grad_bias)


def solution(mesh):
    return jax.shard_map(
        on_device,
        mesh=mesh,
        in_specs=(
            P("dp", None, None),
            P("dp", None),
            P("dp"),
            P("dp"),
            P(None, "mp"),
            P(None, "mp"),
            P("mp"),
            P("dp", None, "mp"),
            P(None, "mp"),
            P("mp"),
            P("mp"),
            P("dp", "mp"),
            P("dp", "mp"),
        ),
        out_specs=(
            P("dp", "mp"),
            P("dp", None, "mp"),
            P("dp", "mp"),
            P(None, "mp"),
            P("mp"),
            P("mp"),
        ),
        check_vma=False,
    )
```
